32 devices in a mesh: row: 4 (over y, x), col: 8 (over z, core).
Axes of the slice: x: 2, y: 2, z: 4, core: 2. Of those that a mesh axis runs over, the one named last changes fastest.
Arguments:
- panel: float32 [3072, 8192], P('row', 'col'), may hold values from -6 to 6
- row_weights: float32 [3072], P('row'), may hold values from 0.25 to 4
Outputs:
- normal_matrix: float32 [8192, 8192], P('row', 'col')
The draws below stay inside these ranges and needn't reach their ends.
All inputs are finite; a program needn't handle non-finite values.
Results may differ from the reference program's by a relative error of at most 0.00011.
Values sent between devices are 32-bit elements; how exact they have to be, the bound alone decides.
No kernel may reach another device: no remote copies, remote signals or barrier semaphores. Data moves between devices by JAX's collectives and lax.ppermute only.
A program may use at most 192 MiB of HBM per device.

```python
import math
import jax
import jax.numpy as jnp
from jax import lax

K = 8192
ROWS = 3072


def block_scale(rng, extent, pieces, smallest, top_value):
    def one(axis_at, shards_of):
        steps = jax.random.uniform(jax.random.fold_in(jax.random.fold_in(rng, 6), axis_at), (shards_of,), jnp.float32, smallest / len(pieces), top_value / len(pieces))
        return jnp.repeat(jnp.exp(steps), extent[axis_at] // shards_of).reshape((-1,) + (1,) * (len(extent) - axis_at - 1))

    loudness = one(*pieces[0])
    for cut in pieces[1:]:
        loudness = loudness * one(*cut)
    return loudness


def scatter_about(rng, shape, scale, limit, pieces=(), kind=jnp.bfloat16):
    loudness = block_scale(rng, shape, pieces, -0.22, 0.18) if pieces else 1.0
    values = jax.random.normal(rng, shape, jnp.float32) * scale * loudness
    return jnp.minimum(jnp.maximum(values, -limit), limit).astype(kind)


def setup_inputs(seed: int = 0) -> dict:
    splits = jax.random.split(jax.random.key(seed), 3)
    return {
        "panel": scatter_about(splits[0], (ROWS, K), 1.0, 6.0, ((0, 4), (1, 8)), jnp.float32),
        "row_weights": jnp.clip(jnp.exp(math.log(4.0) - 2.7725887 * jax.random.uniform(splits[1], (ROWS,), jnp.float32) ** block_scale(splits[1], (ROWS,), ((0, 4),), -0.2, 0.2)), 0.25, 4.0),
    }


def reference(panel, row_weights):
    weighted = row_weights[:, None] * panel
    product = jnp.dot(weighted.T, panel, preferred_element_type=jnp.float32, precision=lax.Precision.HIGHEST)
    return product * (1.0 / ROWS)
```

```python
import jax
import jax.numpy as jnp
from jax import lax
from jax.experimental import pallas as pl
from jax.experimental.pallas import tpu as pltpu
from jax.sharding import PartitionSpec as P

PARTS = (2, 2, 2, 1, 1)
AXES = ("row", "col")


def plain(panel, row_weights):
    total_rows = panel.shape[0] * lax.axis_size("row")
    weighted = row_weights[:, None] * panel
    partial_sum = jnp.dot(
        lax.all_gather(weighted, "col", axis=1, tiled=True).T,
        panel,
        preferred_element_type=jnp.float32,
        precision=lax.Precision.HIGHEST,
    )
    summed = lax.psum_scatter(partial_sum, "row", scatter_dimension=0, tiled=True)
    return summed * (1.0 / total_rows)


def product_body(count, where_ref, mine_ref, other_ref, *refs):
    right_refs, out_ref, hi_ref, lo_ref = refs[:count], refs[-3], refs[-2], refs[-1]
    r, k = where_ref[0], where_ref[1]
    m = mine_ref.shape[1]

    @pl.when(pl.program_id(0) == 0)
    def _():
        for side, ref in enumerate((mine_ref, other_ref)):
            for e in range(count):
                x = ref[lax.bitwise_xor(r, e)]
                hi = x.astype(jnp.bfloat16)
                hi_ref[e, side * m : (side + 1) * m] = hi
                lo_ref[e, side * m : (side + 1) * m] = (x - hi.astype(jnp.float32)).astype(jnp.bfloat16)

    def dot(a, b):
        return jnp.dot(a, b, preferred_element_type=jnp.float32)

    total = None
    for e in range(count):
        right = right_refs[e][...]
        hi = right.astype(jnp.bfloat16)
        lo = (right - hi.astype(jnp.float32)).astype(jnp.bfloat16)
        term = dot(hi_ref[e], hi) + (dot(hi_ref[e], lo) + dot(lo_ref[e], hi))
        total = term if total is None else total + term
    out_ref[k] = total[:m]
    out_ref[1 - k] = total[m:]


def product(where, mine, other, rights, out, start, tile=256):
    count, m, depth = mine.shape
    height = rights[0].shape[1]
    width = rights[0].shape[1]
    assert start % m == 0
    whole_left = pl.BlockSpec((count, m, depth), lambda j, s: (0, 0, 0))
    in_specs = [whole_left, whole_left]
    in_specs += [pl.BlockSpec((depth, tile), lambda j, s: (0, j)) for _ in rights]
    args = [where, mine, other, *rights]
    aliases = {}
    if out is not None:
        in_specs.append(pl.BlockSpec(memory_space=pl.ANY))
        args.append(out)
        aliases = {len(args) - 1: 0}

    def body(where_ref, mine_ref, other_ref, *refs):
        product_body(count, where_ref, mine_ref, other_ref, *refs)

    return pl.pallas_call(
        body,
        out_shape=jax.ShapeDtypeStruct((2, height, width), jnp.float32),
        grid_spec=pltpu.PrefetchScalarGridSpec(
            num_scalar_prefetch=1,
            grid=(width // tile,),
            in_specs=in_specs,
            out_specs=pl.BlockSpec((2, m, tile), lambda j, s: (0, start // m, j)),
            scratch_shapes=[pltpu.VMEM((count, 2 * m, depth), jnp.bfloat16)] * 2,
        ),
        input_output_aliases=aliases,
        compiler_params=pltpu.CompilerParams(vmem_limit_bytes=50 << 20),
        cost_estimate=pl.CostEstimate(
            flops=6 * 2 * m * width * depth * count,
            bytes_accessed=4 * (2 * count * m * depth + count * depth * width + 2 * m * width),
            transcendentals=0,
        ),
    )(*args)


def exchange(panel, row_weights):
    n = lax.axis_size("row")
    cols = lax.axis_size("col")
    r = lax.axis_index("row")
    k = lax.axis_index("col") % 2
    where = jnp.stack([r, k]).astype(jnp.int32)
    rows, width = panel.shape

    def across(x, e):
        moves = [(a * cols + b, (a ^ e) * cols + b) for a in range(n) for b in range(cols)]
        return lax.ppermute(x, AXES, moves)

    def swap(x):
        moves = [(a * cols + b, a * cols + (b ^ 1)) for a in range(n) for b in range(cols)]
        return lax.ppermute(x, AXES, moves)

    scale = jnp.sqrt(row_weights * (1.0 / (rows * n)))
    own = panel * scale[:, None]

    rights = [own]
    half = width // 2
    for e in range(1, n):
        top = 1 << (e.bit_length() - 1)
        low = e & -e
        if top == low:
            rights.append(across(own, e))
        else:
            parts = [across(rights[e ^ top][:, :half], top), across(rights[e ^ low][:, half:], low)]
            rights.append(jnp.concatenate(parts, axis=1))

    groups = [[b for b in range(cols) if b % 2 == core] for core in (0, 1)]
    unit = width // sum(PARTS)
    starts = [unit * sum(PARTS[:i]) for i in range(len(PARTS))]
    outs, arrived = [None], []

    def finish(i):
        outs.append(product(where, arrived[i], swap(arrived[i]), rights, outs[-1], starts[i]))

    for i, part in enumerate(PARTS):
        piece = lax.slice_in_dim(panel, starts[i], starts[i] + part * unit, axis=1).T * scale
        if i >= 2:
            piece, arrived[i - 2] = lax.optimization_barrier((piece, arrived[i - 2]))
        if i == 2:
            piece, rights[:3] = lax.optimization_barrier((piece, rights[:3]))
        if i == 3:
            piece, rights = lax.optimization_barrier((piece, rights))
        line = lax.all_gather(piece, "col", axis=0, axis_index_groups=groups)
        if i >= 2:
            finish(i - 2)
            line, outs[-1] = lax.optimization_barrier((line, outs[-1]))
        arrived.append(lax.all_to_all(line, "row", 0, 0))
    for i in range(len(PARTS) - 2, len(PARTS)):
        finish(i)
    out = outs[-1]
    return out.reshape(2 * width, width)


def solution(mesh):
    n, cols = mesh.shape["row"], mesh.shape["col"]
    paired = cols == 2 * n and n & (n - 1) == 0 and n > 1
    return jax.shard_map(
        exchange if paired else plain,
        mesh=mesh,
        in_specs=(P("row", "col"), P("row")),
        out_specs=P("row", "col"),
        check_vma=False,
    )
```

```python
import jax
import jax.numpy as jnp
from jax import lax
from jax.experimental import pallas as pl
from jax.experimental.pallas import tpu as pltpu
from jax.sharding import PartitionSpec as P

PARTS = (2, 2, 2, 1, 1)
AXES = ("row", "col")


def plain(panel, row_weights):
    total_rows = panel.shape[0] * lax.axis_size("row")
    weighted = row_weights[:, None] * panel
    partial_sum = jnp.dot(
        lax.all_gather(weighted, "col", axis=1, tiled=True).T,
        panel,
        preferred_element_type=jnp.float32,
        precision=lax.Precision.HIGHEST,
    )
    summed = lax.psum_scatter(partial_sum, "row", scatter_dimension=0, tiled=True)
    return summed * (1.0 / total_rows)


def product_body(where_ref, mine_ref, other_ref, high_ref, low_ref, *refs):
    out_ref, left_high, left_low = refs[-3:]
    k, e = where_ref[1], pl.program_id(0)
    m, width = mine_ref.shape[1], high_ref.shape[2]
    for side, ref in enumerate((mine_ref, other_ref)):
        x = ref[0]
        high = x.astype(jnp.bfloat16)
        left_high[side * m : (side + 1) * m] = high
        left_low[side * m : (side + 1) * m] = (x - high.astype(jnp.float32)).astype(jnp.bfloat16)

    def dot(a, b):
        return jnp.dot(a[...], b, preferred_element_type=jnp.float32)

    tile = min(256, width)
    for j in range(0, width, tile):
        high, low = high_ref[0, :, j : j + tile], low_ref[0, :, j : j + tile]
        total = dot(left_high, high) + (dot(left_high, low) + dot(left_low, high))
        for side, place in enumerate((k, 1 - k)):
            part = total[side * m : (side + 1) * m]
            before = out_ref[place, :, j : j + tile]
            out_ref[place, :, j : j + tile] = jnp.where(e == 0, part, before + part)


def product(where, mine, other, right, out, start):
    count, m, depth = mine.shape
    height = width = right[0].shape[2]
    assert start % m == 0
    left_spec = pl.BlockSpec((1, m, depth), lambda e, s: (s[0] ^ e, 0, 0))
    right_spec = pl.BlockSpec((1, depth, width), lambda e, s: (e, 0, 0))
    in_specs = [left_spec, left_spec, right_spec, right_spec]
    args = [where, mine, other, *right]
    aliases = {}
    if out is not None:
        in_specs.append(pl.BlockSpec(memory_space=pl.ANY))
        args.append(out)
        aliases = {len(args) - 1: 0}
    return pl.pallas_call(
        product_body,
        out_shape=jax.ShapeDtypeStruct((2, height, width), jnp.float32),
        grid_spec=pltpu.PrefetchScalarGridSpec(
            num_scalar_prefetch=1,
            grid=(count,),
            in_specs=in_specs,
            out_specs=pl.BlockSpec((2, m, width), lambda e, s: (0, start // m, 0)),
            scratch_shapes=[pltpu.VMEM((2 * m, depth), jnp.bfloat16)] * 2,
        ),
        input_output_aliases=aliases,
        compiler_params=pltpu.CompilerParams(vmem_limit_bytes=50 << 20),
        cost_estimate=pl.CostEstimate(
            flops=6 * 2 * m * width * depth * count,
            bytes_accessed=4 * (2 * count * m * depth + count * depth * width + 2 * m * width),
            transcendentals=0,
        ),
    )(*args)


def split(rights):
    whole = jnp.stack(rights)
    high = lax.reduce_precision(whole, 8, 7)
    return high.astype(jnp.bfloat16), (whole - high).astype(jnp.bfloat16)


def exchange(panel, row_weights):
    n = lax.axis_size("row")
    cols = lax.axis_size("col")
    r = lax.axis_index("row")
    k = lax.axis_index("col") % 2
    where = jnp.stack([r, k]).astype(jnp.int32)
    rows, width = panel.shape

    def across(x, e):
        moves = [(a * cols + b, (a ^ e) * cols + b) for a in range(n) for b in range(cols)]
        return lax.ppermute(x, AXES, moves)

    def swap(x):
        moves = [(a * cols + b, a * cols + (b ^ 1)) for a in range(n) for b in range(cols)]
        return lax.ppermute(x, AXES, moves)

    scale = jnp.sqrt(row_weights * (1.0 / (rows * n)))
    own = panel * scale[:, None]

    rights = [own]
    half = width // 2
    for e in range(1, n):
        top = 1 << (e.bit_length() - 1)
        low = e & -e
        if top == low:
            rights.append(across(own, e))
        else:
            parts = [across(rights[e ^ top][:, :half], top), across(rights[e ^ low][:, half:], low)]
            rights.append(jnp.concatenate(parts, axis=1))

    groups = [[b for b in range(cols) if b % 2 == core] for core in (0, 1)]
    unit = width // sum(PARTS)
    starts = [unit * sum(PARTS[:i]) for i in range(len(PARTS))]
    last = len(PARTS) - 1
    right = split(rights)
    outs, blocks = [None], []

    def finish(i):
        outs.append(product(where, blocks[i], swap(blocks[i]), right, outs[-1], starts[i]))

    for i, part in enumerate(PARTS):
        piece = lax.slice_in_dim(panel, starts[i], starts[i] + part * unit, axis=1).T * scale
        if i >= 2:
            piece, blocks[i - 2] = lax.optimization_barrier((piece, blocks[i - 2]))
        if i == 2:
            piece, rights[:3] = lax.optimization_barrier((piece, rights[:3]))
        if i == 3:
            piece, rights = lax.optimization_barrier((piece, rights))
        line = lax.all_gather(piece, "col", axis=0, axis_index_groups=groups)
        for done in {2: [0]}.get(i, []):
            finish(done)
            line, outs[-1] = lax.optimization_barrier((line, outs[-1]))
        block = lax.all_to_all(line, "row", 0, 0)
        for done in {3: [1, 2], 4: [3]}.get(i, []):
            finish(done)
            block, outs[-1] = lax.optimization_barrier((block, outs[-1]))
        blocks.append(block)
    finish(last)
    out = outs[-1]
    return out.reshape(2 * width, width)


def solution(mesh):
    n, cols = mesh.shape["row"], mesh.shape["col"]
    paired = cols == 2 * n and n & (n - 1) == 0 and n > 1
    return jax.shard_map(
        exchange if paired else plain,
        mesh=mesh,
        in_specs=(P("row", "col"), P("row")),
        out_specs=P("row", "col"),
        check_vma=False,
    )
```

```python
import jax
import jax.numpy as jnp
from jax import lax
from jax.experimental import pallas as pl
from jax.experimental.pallas import tpu as pltpu
from jax.sharding import PartitionSpec as P

PARTS = (2, 2, 2, 1, 1)
AXES = ("row", "col")


def plain(panel, row_weights):
    total_rows = panel.shape[0] * lax.axis_size("row")
    weighted = row_weights[:, None] * panel
    partial_sum = jnp.dot(
        lax.all_gather(weighted, "col", axis=1, tiled=True).T,
        panel,
        preferred_element_type=jnp.float32,
        precision=lax.Precision.HIGHEST,
    )
    summed = lax.psum_scatter(partial_sum, "row", scatter_dimension=0, tiled=True)
    return summed * (1.0 / total_rows)


def product_body(where_ref, mine_ref, other_ref, high_ref, low_ref, *refs):
    out_ref, left_high, left_low = refs[-3:]
    k, e = where_ref[1], pl.program_id(0)
    m, width = mine_ref.shape[1], high_ref.shape[2]
    for side, ref in enumerate((mine_ref, other_ref)):
        x = ref[0]
        high = x.astype(jnp.bfloat16)
        left_high[side * m : (side + 1) * m] = high
        left_low[side * m : (side + 1) * m] = (x - high.astype(jnp.float32)).astype(jnp.bfloat16)

    def dot(a, b):
        return jnp.dot(a[...], b, preferred_element_type=jnp.float32)

    tile = min(256, width)
    for j in range(0, width, tile):
        high, low = high_ref[0, :, j : j + tile], low_ref[0, :, j : j + tile]
        total = dot(left_high, high) + (dot(left_high, low) + dot(left_low, high))
        for side, place in enumerate((k, 1 - k)):
            part = total[side * m : (side + 1) * m]
            before = out_ref[place, :, j : j + tile]
            out_ref[place, :, j : j + tile] = jnp.where(e == 0, part, before + part)


def product(where, mine, other, right, out, start):
    count, m, depth = mine.shape
    height = width = right[0].shape[2]
    assert start % m == 0
    left_spec = pl.BlockSpec((1, m, depth), lambda e, s: (s[0] ^ e, 0, 0))
    right_spec = pl.BlockSpec((1, depth, width), lambda e, s: (e, 0, 0))
    in_specs = [left_spec, left_spec, right_spec, right_spec]
    args = [where, mine, other, *right]
    aliases = {}
    if out is not None:
        in_specs.append(pl.BlockSpec(memory_space=pl.ANY))
        args.append(out)
        aliases = {len(args) - 1: 0}
    return pl.pallas_call(
        product_body,
        out_shape=jax.ShapeDtypeStruct((2, height, width), jnp.float32),
        grid_spec=pltpu.PrefetchScalarGridSpec(
            num_scalar_prefetch=1,
            grid=(count,),
            in_specs=in_specs,
            out_specs=pl.BlockSpec((2, m, width), lambda e, s: (0, start // m, 0)),
            scratch_shapes=[pltpu.VMEM((2 * m, depth), jnp.bfloat16)] * 2,
        ),
        input_output_aliases=aliases,
        compiler_params=pltpu.CompilerParams(vmem_limit_bytes=50 << 20),
        cost_estimate=pl.CostEstimate(flops=4 * m * width * depth, bytes_accessed=8 * m * width, transcendentals=0),
    )(*args)


def split(rights):
    whole = jnp.stack(rights)
    high = lax.reduce_precision(whole, 8, 7)
    return high.astype(jnp.bfloat16), (whole - high).astype(jnp.bfloat16)


def exchange(panel, row_weights):
    n = lax.axis_size("row")
    cols = lax.axis_size("col")
    r = lax.axis_index("row")
    k = lax.axis_index("col") % 2
    where = jnp.stack([r, k]).astype(jnp.int32)
    rows, width = panel.shape

    def across(x, e):
        moves = [(a * cols + b, (a ^ e) * cols + b) for a in range(n) for b in range(cols)]
        return lax.ppermute(x, AXES, moves)

    def swap(x):
        moves = [(a * cols + b, a * cols + (b ^ 1)) for a in range(n) for b in range(cols)]
        return lax.ppermute(x, AXES, moves)

    scale = jnp.sqrt(row_weights * (1.0 / (rows * n)))
    own = panel * scale[:, None]

    rights = [own]
    half = width // 2
    for e in range(1, n):
        top = 1 << (e.bit_length() - 1)
        low = e & -e
        if top == low:
            rights.append(across(own, e))
        else:
            parts = [across(rights[e ^ top][:, :half], top), across(rights[e ^ low][:, half:], low)]
            rights.append(jnp.concatenate(parts, axis=1))

    groups = [[b for b in range(cols) if b % 2 == core] for core in (0, 1)]
    unit = width // sum(PARTS)
    starts = [unit * sum(PARTS[:i]) for i in range(len(PARTS))]
    last = len(PARTS) - 1
    right = split(rights)
    outs, blocks = [None], []

    def finish(i):
        outs.append(product(where, blocks[i], swap(blocks[i]), right, outs[-1], starts[i]))

    for i, part in enumerate(PARTS):
        piece = lax.slice_in_dim(panel, starts[i], starts[i] + part * unit, axis=1).T * scale
        if i >= 2:
            piece, blocks[i - 2] = lax.optimization_barrier((piece, blocks[i - 2]))
        if i == 2:
            piece, rights[:3] = lax.optimization_barrier((piece, rights[:3]))
        if i == 3:
            piece, rights = lax.optimization_barrier((piece, rights))
        line = lax.all_gather(piece, "col", axis=0, axis_index_groups=groups)
        for done in {2: [0]}.get(i, []):
            finish(done)
            line, outs[-1] = lax.optimization_barrier((line, outs[-1]))
        block = lax.all_to_all(line, "row", 0, 0)
        for done in {3: [1, 2], 4: [3]}.get(i, []):
            finish(done)
            block, outs[-1] = lax.optimization_barrier((block, outs[-1]))
        blocks.append(block)
    finish(last)
    out = outs[-1]
    return out.reshape(2 * width, width)


def solution(mesh):
    n, cols = mesh.shape["row"], mesh.shape["col"]
    paired = cols == 2 * n and n & (n - 1) == 0 and n > 1
    return jax.shard_map(
        exchange if paired else plain,
        mesh=mesh,
        in_specs=(P("row", "col"), P("row")),
        out_specs=P("row", "col"),
        check_vma=False,
    )
```

```python
import jax
import jax.numpy as jnp
from jax import lax
from jax.experimental import pallas as pl
from jax.experimental.pallas import tpu as pltpu
from jax.sharding import PartitionSpec as P

PARTS = ((4, 2), (0, 3), (6, 2), (3, 1))
AXES = ("row", "col")


def plain(panel, row_weights):
    total_rows = panel.shape[0] * lax.axis_size("row")
    weighted = row_weights[:, None] * panel
    partial_sum = jnp.dot(
        lax.all_gather(weighted, "col", axis=1, tiled=True).T,
        panel,
        preferred_element_type=jnp.float32,
        precision=lax.Precision.HIGHEST,
    )
    summed = lax.psum_scatter(partial_sum, "row", scatter_dimension=0, tiled=True)
    return summed * (1.0 / total_rows)


def product_body(where_ref, mine_ref, other_ref, high_ref, low_ref, *refs):
    out_ref, left_high, left_low = refs[-3:]
    k, e = where_ref[1], pl.program_id(0)
    m, width = mine_ref.shape[1], high_ref.shape[2]
    for side, ref in enumerate((mine_ref, other_ref)):
        x = ref[0]
        high = x.astype(jnp.bfloat16)
        left_high[side * m : (side + 1) * m] = high
        left_low[side * m : (side + 1) * m] = (x - high.astype(jnp.float32)).astype(jnp.bfloat16)

    def dot(a, b):
        return jnp.dot(a[...], b, preferred_element_type=jnp.float32)

    tile = min(256, width)
    for j in range(0, width, tile):
        high, low = high_ref[0, :, j : j + tile], low_ref[0, :, j : j + tile]
        total = dot(left_high, high) + (dot(left_high, low) + dot(left_low, high))
        for side, place in enumerate((k, 1 - k)):
            part = total[side * m : (side + 1) * m]
            before = out_ref[place, :, j : j + tile]
            out_ref[place, :, j : j + tile] = jnp.where(e == 0, part, before + part)


def product(where, mine, other, right, out, start):
    count, m, depth = mine.shape
    height = width = right[0].shape[2]
    assert start % m == 0
    left_spec = pl.BlockSpec((1, m, depth), lambda e, s: (s[0] ^ e, 0, 0))
    right_spec = pl.BlockSpec((1, depth, width), lambda e, s: (e, 0, 0))
    in_specs = [left_spec, left_spec, right_spec, right_spec]
    args = [where, mine, other, *right]
    aliases = {}
    if out is not None:
        in_specs.append(pl.BlockSpec(memory_space=pl.ANY))
        args.append(out)
        aliases = {len(args) - 1: 0}
    return pl.pallas_call(
        product_body,
        out_shape=jax.ShapeDtypeStruct((2, height, width), jnp.float32),
        grid_spec=pltpu.PrefetchScalarGridSpec(
            num_scalar_prefetch=1,
            grid=(count,),
            in_specs=in_specs,
            out_specs=pl.BlockSpec((2, m, width), lambda e, s: (0, start // m, 0)),
            scratch_shapes=[pltpu.VMEM((2 * m, depth), jnp.bfloat16)] * 2,
        ),
        input_output_aliases=aliases,
        compiler_params=pltpu.CompilerParams(vmem_limit_bytes=50 << 20),
        cost_estimate=pl.CostEstimate(flops=4 * m * width * depth, bytes_accessed=8 * m * width, transcendentals=0),
    )(*args)


def split(rights):
    whole = jnp.stack(rights)
    high = lax.reduce_precision(whole, 8, 7)
    return high.astype(jnp.bfloat16), (whole - high).astype(jnp.bfloat16)


def exchange(panel, row_weights):
    n = lax.axis_size("row")
    cols = lax.axis_size("col")
    r = lax.axis_index("row")
    k = lax.axis_index("col") % 2
    where = jnp.stack([r, k]).astype(jnp.int32)
    rows, width = panel.shape

    def across(x, e):
        moves = [(a * cols + b, (a ^ e) * cols + b) for a in range(n) for b in range(cols)]
        return lax.ppermute(x, AXES, moves)

    def swap(x):
        moves = [(a * cols + b, a * cols + (b ^ 1)) for a in range(n) for b in range(cols)]
        return lax.ppermute(x, AXES, moves)

    scale = jnp.sqrt(row_weights * (1.0 / (rows * n)))
    own = panel * scale[:, None]

    rights = [own]
    half = width // 2
    for e in range(1, n):
        top = 1 << (e.bit_length() - 1)
        low = e & -e
        if top == low:
            rights.append(across(own, e))
        else:
            parts = [across(rights[e ^ top][:, :half], top), across(rights[e ^ low][:, half:], low)]
            rights.append(jnp.concatenate(parts, axis=1))

    groups = [[b for b in range(cols) if b % 2 == core] for core in (0, 1)]
    unit = width // sum(part for _, part in PARTS)
    starts = [start * unit for start, _ in PARTS]
    last = len(PARTS) - 1
    right = split(rights)
    outs, blocks = [None], []

    def finish(i):
        outs.append(product(where, blocks[i], swap(blocks[i]), right, outs[-1], starts[i]))

    for i, (_, part) in enumerate(PARTS):
        piece = lax.slice_in_dim(panel, starts[i], starts[i] + part * unit, axis=1).T * scale
        if i >= 2:
            piece, blocks[i - 2] = lax.optimization_barrier((piece, blocks[i - 2]))
        if i == 2:
            piece, rights[:3] = lax.optimization_barrier((piece, rights[:3]))
        if i == 3:
            piece, rights = lax.optimization_barrier((piece, rights))
        line = lax.all_gather(piece, "col", axis=0, axis_index_groups=groups)
        for done in {2: [0]}.get(i, []):
            finish(done)
            line, outs[-1] = lax.optimization_barrier((line, outs[-1]))
        block = lax.all_to_all(line, "row", 0, 0)
        for done in {2: [1], 3: [2]}.get(i, []):
            finish(done)
            block, outs[-1] = lax.optimization_barrier((block, outs[-1]))
        blocks.append(block)
    finish(last)
    out = outs[-1]
    return out.reshape(2 * width, width)


def solution(mesh):
    n, cols = mesh.shape["row"], mesh.shape["col"]
    paired = cols == 2 * n and n & (n - 1) == 0 and n > 1
    return jax.shard_map(
        exchange if paired else plain,
        mesh=mesh,
        in_specs=(P("row", "col"), P("row")),
        out_specs=P("row", "col"),
        check_vma=False,
    )
```
